256 devices in a mesh: replica: 8 (over z_lo, core), fsdp: 32 (over y, x, z_hi).
Axes of the slice: x: 4, y: 4, z: 8 (z_hi: 2, z_lo: 4; z = z_hi * 4 + z_lo), core: 2. Of those that a mesh axis runs over, the one named last changes fastest.
Arguments:
- tok_inputs: bfloat16 [8, 8192, 256], P('replica', 'fsdp'), may hold values from -6 to 6
- tok_grads: bfloat16 [8, 8192, 14336], P('replica', 'fsdp'), may hold values from -0.0625 to 0.0625
- inner_params: float32 [8, 256, 14336], P('replica', 'fsdp'), may hold values from -4 to 4
- adam_first: float32 [8, 256, 14336], P('replica', 'fsdp'), may hold values from -3 to 3
- adam_second: float32 [8, 256, 14336], P('replica', 'fsdp'), may hold values from 0.05 to 1
- global_params: float32 [256, 14336], P('fsdp'), may hold values from -4 to 4
- outer_momentum: float32 [256, 14336], P('fsdp'), may hold values from -3 to 3
Outputs:
- first_moment: float32 [8, 256, 14336], P('replica', 'fsdp')
- second_moment: float32 [8, 256, 14336], P('replica', 'fsdp')
- global_next: float32 [256, 14336], P('fsdp')
- momentum_next: float32 [256, 14336], P('fsdp')
The draws below stay inside these ranges and needn't reach their ends.
All inputs are finite; a program needn't handle non-finite values.
Results may differ from the reference program's by a relative error of at most 0.0003.
Values may be sent and summed in bfloat16 or wider, within the bound.
A program may use at most 128 MiB of HBM per device.

```python
import math
import jax
import jax.numpy as jnp
from jax import lax

FF = 14336
REPLICAS = 8
TOKENS = 8192
D_WIN = 256


def strengthened(result, own_key, source, target, blocks, factor):
    owner, partner = [(jnp.arange(result.shape[dim]) // (result.shape[dim] // blocks)).reshape([-1 if axis == dim else 1 for axis in range(result.ndim)]) for dim in (source, target)]
    chosen = jax.random.permutation(own_key, blocks)[partner]
    strong = (owner == chosen) | (owner == (partner + blocks // 2) % blocks)
    return jnp.where(strong, factor * result, result)


def levels(own_key, dims, cuts, low, top_value):
    level = 1.0
    for axis_at, shards_of in cuts:
        heights = jax.random.uniform(jax.random.fold_in(jax.random.fold_in(own_key, 6), axis_at), (shards_of,), jnp.float32, low / len(cuts), top_value / len(cuts))
        level = level * jnp.repeat(jnp.exp(heights), dims[axis_at] // shards_of).reshape((-1,) + (1,) * (len(dims) - 1 - axis_at))
    return level


def bell_draw(own_key, dims, spread, most, split=(), dtype=jnp.bfloat16):
    entries = jax.random.normal(own_key, dims, jnp.float32) * spread
    if len(split) > 0:
        entries = levels(own_key, dims, split, -0.22, 0.18) * entries
    return jnp.clip(entries, min=-most, max=most).astype(dtype)


def bell_draw_with(rng, dims, scale, bound, pieces, heavy, kind=jnp.bfloat16):
    values = scale * jax.random.normal(rng, dims, jnp.float32)
    if pieces:
        values = values * levels(rng, dims, pieces, -0.22, 0.18)
    return jnp.clip(strengthened(values, jax.random.fold_in(rng, 3), *heavy), -bound, bound).astype(kind)


def setup_inputs(seed: int = 0) -> dict:
    splits = jax.random.split(jax.random.key(seed), 8)
    return {
        "tok_inputs": bell_draw_with(splits[0], (REPLICAS, TOKENS, D_WIN), 1.0, 6.0, ((0, 8), (1, 32)), (1, 2, 32, 2.75)),
        "tok_grads": bell_draw(splits[1], (REPLICAS, TOKENS, FF), TOKENS ** -0.5, 0.0625, ((0, 8), (1, 32))),
        "inner_params": bell_draw(splits[2], (REPLICAS, D_WIN, FF), 0.5, 4.0, ((0, 8), (1, 32)), jnp.float32),
        "adam_first": bell_draw(splits[3], (REPLICAS, D_WIN, FF), 0.3, 3.0, ((0, 8), (1, 32)), jnp.float32),
        "adam_second": jnp.clip(jnp.exp(math.log(1.0) - 2.9957323 * jax.random.uniform(splits[4], (REPLICAS, D_WIN, FF), jnp.float32) ** levels(splits[4], (REPLICAS, D_WIN, FF), ((0, 8), (1, 32)), -0.2, 0.2)), 0.05, 1.0),
        "global_params": bell_draw(splits[5], (D_WIN, FF), 0.5, 4.0, ((0, 32),), jnp.float32),
        "outer_momentum": bell_draw(splits[6], (D_WIN, FF), 0.3, 3.0, ((0, 32),), jnp.float32),
    }


beta_first = 0.9
beta_second = 0.95
inner_rate = 0.1
outer_rate = 0.7
momentum_decay = 0.9
epsilon = 1e-08
first_correction = 1.0 - 0.9 ** 40
second_correction = 1.0 - 0.95 ** 40

def replica_gradient(pair):
    inputs, grads = pair
    return jnp.dot(inputs.T, grads, preferred_element_type=jnp.float32)

def reference(tok_inputs, tok_grads, inner_params, adam_first, adam_second, global_params, outer_momentum):
    gradient = lax.map(replica_gradient, (tok_inputs, tok_grads))
    first_moment = beta_first * adam_first + (1.0 - beta_first) * gradient
    second_moment = beta_second * adam_second + (1.0 - beta_second) * gradient * gradient
    update = first_moment / first_correction / (jnp.sqrt(second_moment / second_correction) + epsilon)
    inner_next = inner_params - inner_rate * update
    pseudo = global_params[None] - inner_next
    average = lax.optimization_barrier(jnp.sum(pseudo, axis=0)) / REPLICAS
    momentum_next = momentum_decay * outer_momentum + average
    global_next = global_params - outer_rate * (average + momentum_decay * momentum_next)
    return (first_moment, second_moment, global_next, momentum_next)
```

```python
import functools
import jax
import jax.numpy as jnp
from jax import lax
from jax.experimental import pallas as pl
from jax.experimental.pallas import tpu as pltpu
from jax.sharding import PartitionSpec as P

beta_first = 0.9
beta_second = 0.95
inner_rate = 0.1
outer_rate = 0.7
momentum_decay = 0.9
epsilon = 1e-08
first_correction = 1.0 - 0.9**40
second_correction = 1.0 - 0.95**40

MESH = pl.DeviceIdType.MESH
SIDE = 4
WIDE = 1024
HALF = WIDE // 2
PIECE = WIDE // SIDE
POWER = 7
SCALES = (10, 8, 7)


def encode(value, stage):
    u = value * (2.0 ** SCALES[stage])
    u2 = u * u
    return (u2 * u2 * (u2 * u)).astype(jnp.bfloat16)


def decode_add(total, code, stage):
    y = code.astype(jnp.float32)
    size = jnp.exp2(jnp.log2(jnp.abs(y)) * (1.0 / POWER) - SCALES[stage])
    return jnp.where(y < 0, total - size, total + size)


def kernel(
    feat_ref, g_hbm, p_hbm, a1_hbm, a2_hbm, w_hbm, m_hbm,
    fm_ref, sm_ref, gn_ref, mn_ref,
    feat_t, g_ref, par, part, s1, r1, s2, r2, sz, rz, pse, mrecv, ssum, lrecv, tot,
    g_sem, par_sem, xy_send, xy_recv, z_send, z_recv, m_send, m_recv, l_send, l_recv, b_send, b_recv,
):
    ff = g_ref.shape[1]
    fh = ff // 2
    chunks = fh // WIDE
    rep = lax.axis_index("replica")
    fs = lax.axis_index("fsdp")
    q, k = rep // 2, rep % 2
    pos = (fs // 8, (fs // 2) % SIDE)
    zh = fs % 2
    zpeer = (rep, fs + 1 - 2 * zh)
    mate = (rep + 1 - 2 * k, fs)

    def ring(axis, step):
        y, x = pos
        if axis == 0:
            y = (y + step) % SIDE
        else:
            x = (x + step) % SIDE
        return (rep, y * 8 + x * 2 + zh)

    def start_col(c, h):
        return pl.multiple_of(h * fh + c * WIDE, WIDE)

    def g_copy(c, h):
        cols = pl.ds(start_col(c, h), WIDE)
        return pltpu.make_async_copy(g_hbm.at[:, cols], g_ref.at[:, cols], g_sem.at[c, h])

    par_copies = [
        pltpu.make_async_copy(src, par.at[i], par_sem.at[i])
        for i, src in enumerate((p_hbm, a1_hbm, a2_hbm, w_hbm, m_hbm))
    ]
    for h in range(2):
        g_copy(0, h).start()

    barrier = pltpu.get_barrier_semaphore()
    peers = [ring(a, s) for a in range(2) for s in (1, 3)] + [zpeer]
    peers += [((rep + d) % 8, fs) for d in range(1, 8)]
    for peer in peers:
        pl.semaphore_signal(barrier, inc=1, device_id=peer, device_id_type=MESH)

    @pl.loop(1, chunks)
    def _(c):
        for h in range(2):
            g_copy(c, h).start()

    for copy in par_copies:
        copy.start()

    feat_t[0] = feat_ref[...].astype(jnp.float32).T.astype(jnp.bfloat16)
    for y in range(SIDE):
        for x in range(SIDE):
            feat_t[1, pl.ds((x * SIDE + y) * 16, 16), :] = feat_t[0, pl.ds((y * SIDE + x) * 16, 16), :]

    def xy_copy(c, h, p, d, m):
        send, recv = ((s1, r1), (s2, r2))[p]
        slots = pl.ds(0, 2) if m == 0 else pl.ds(2, 1)
        return pltpu.make_async_remote_copy(
            src_ref=send.at[c, h, d, slots],
            dst_ref=recv.at[c, h, d, slots],
            send_sem=xy_send.at[c, ((h * 2 + p) * 2 + d) * 2 + m],
            recv_sem=xy_recv.at[c, ((h * 2 + p) * 2 + d) * 2 + m],
            device_id=ring((h + p) % 2, 1 if d == 0 else SIDE - 1),
            device_id_type=MESH,
        )

    def z_copy(c):
        return pltpu.make_async_remote_copy(
            src_ref=sz.at[c], dst_ref=rz.at[c], send_sem=z_send.at[c], recv_sem=z_recv.at[c],
            device_id=zpeer, device_id_type=MESH,
        )

    def m_copy(c):
        return pltpu.make_async_remote_copy(
            src_ref=pse.at[c, 1 - k], dst_ref=mrecv.at[c], send_sem=m_send.at[c], recv_sem=m_recv.at[c],
            device_id=mate, device_id_type=MESH,
        )

    def l_copy(c, d):
        to = (q + d) % SIDE
        return pltpu.make_async_remote_copy(
            src_ref=ssum.at[c, to], dst_ref=lrecv.at[c, d - 1],
            send_sem=l_send.at[c, d - 1], recv_sem=l_recv.at[c, d - 1],
            device_id=(to * 2 + k, fs), device_id_type=MESH,
        )

    def b_copy(c, d):
        return pltpu.make_async_remote_copy(
            src_ref=tot.at[c, 0], dst_ref=tot.at[c, d],
            send_sem=b_send.at[c, d - 1], recv_sem=b_recv.at[c, d - 1],
            device_id=((rep + d) % 8, fs), device_id_type=MESH,
        )

    def places(c, h, p):
        j = pos[(h + p) % 2]
        right = pl.ds(start_col(c, h), HALF)
        left = pl.ds(pl.multiple_of(start_col(c, h) + HALF, HALF), HALF)

        def at(dest, i, cols):
            dest = dest % SIDE
            return (dest, i, slice(None), cols) if p == 0 else (pos[h], dest, slice(None), cols)

        return j, right, left, at

    def over_blocks(p, body):
        if p == 0:
            pl.loop(0, SIDE)(body)
        else:
            body(0)

    def first_sends(c, h, p):
        send = (s1, s2)[p]
        j, right, left, at = places(c, h, p)

        def body(i):
            send[c, h, 0, 0, i] = encode(part[at(j + 2, i, right)], p)
            send[c, h, 0, 1, i] = encode(part[at(j + 1, i, left)], p)
            send[c, h, 1, 0, i] = encode(part[at(j + 2, i, left)], p)
            send[c, h, 1, 1, i] = encode(part[at(j + 3, i, right)], p)

        over_blocks(p, body)
        for d in range(2):
            xy_copy(c, h, p, d, 0).start()

    def second_sends(c, h, p):
        send, recv = ((s1, r1), (s2, r2))[p]
        j, right, left, at = places(c, h, p)
        for d in range(2):
            xy_copy(c, h, p, d, 0).wait_recv()

        def body(i):
            send[c, h, 0, 2, i] = encode(decode_add(part[at(j + 1, i, right)], recv[c, h, 0, 0, i], p), p)
            send[c, h, 1, 2, i] = encode(decode_add(part[at(j + 3, i, left)], recv[c, h, 1, 0, i], p), p)

        over_blocks(p, body)
        for d in range(2):
            xy_copy(c, h, p, d, 1).start()

    def collect(c, h, p):
        recv = (r1, r2)[p]
        j, right, left, at = places(c, h, p)
        for d in range(2):
            xy_copy(c, h, p, d, 1).wait_recv()

        def body(i):
            part[at(j, i, right)] = decode_add(
                decode_add(part[at(j, i, right)], recv[c, h, 0, 2, i], p), recv[c, h, 1, 1, i], p
            )
            part[at(j, i, left)] = decode_add(
                decode_add(part[at(j, i, left)], recv[c, h, 0, 1, i], p), recv[c, h, 1, 2, i], p
            )

        over_blocks(p, body)

    def multiply(c, h):
        g_copy(c, h).wait()

        @pl.loop(0, WIDE // 256)
        def _(t):
            cols = pl.ds(pl.multiple_of(start_col(c, h) + t * 256, 256), 256)
            part[:, :, :, cols] = jnp.dot(
                feat_t[h], g_ref[:, cols], preferred_element_type=jnp.float32
            ).reshape(SIDE, SIDE, 16, 256)

    def rows_of(h, whose, cols):
        return (pos[h], pos[1 - h], pl.ds(pl.multiple_of(whose * 8, 8), 8), cols)

    def stage0(c):
        for h in range(2):
            multiply(c, h)

            if h == 0:
                @pl.when(c == 0)
                def _():
                    pl.semaphore_wait(barrier, len(peers))

            first_sends(c, h, 0)

    def stage1(c):
        for h in range(2):
            second_sends(c, h, 0)

    def stage2(c):
        for h in range(2):
            collect(c, h, 0)
            first_sends(c, h, 1)

    def stage3(c):
        for h in range(2):
            second_sends(c, h, 1)

    def stage4(c):
        for h in range(2):
            collect(c, h, 1)

        @pl.loop(0, WIDE // HALF)
        def _(t):
            both = [
                part[rows_of(h, 1 - zh, pl.ds(pl.multiple_of(start_col(c, h) + t * HALF, HALF), HALF))]
                for h in range(2)
            ]
            sz[c, :, pl.ds(pl.multiple_of(t * HALF, HALF), HALF)] = encode(jnp.concatenate(both, axis=0), 2)

        z_copy(c).start()

    def stage5(c):
        @pl.when(c == 0)
        def _():
            for copy in par_copies:
                copy.wait()

        z_copy(c).wait_recv()

        @pl.loop(0, WIDE // HALF)
        def _(t):
            sub = pl.ds(pl.multiple_of(t * HALF, HALF), HALF)
            cols = [pl.ds(pl.multiple_of(start_col(c, h) + t * HALF, HALF), HALF) for h in range(2)]
            both = jnp.concatenate([part[rows_of(h, zh, cols[h])] for h in range(2)], axis=0)
            both = decode_add(both, rz[c, :, sub], 2)
            for h in range(2):
                gradient = both[h * 8 : h * 8 + 8]
                first = beta_first * par[1, :, cols[h]] + (1.0 - beta_first) * gradient
                second = beta_second * par[2, :, cols[h]] + (1.0 - beta_second) * gradient * gradient
                fm_ref[:, cols[h]] = first
                sm_ref[:, cols[h]] = second
                update = first / first_correction / (jnp.sqrt(second / second_correction) + epsilon)
                pse[c, h, :, sub] = par[3, :, cols[h]] - (par[0, :, cols[h]] - inner_rate * update)

        m_copy(c).start()

    def stage6(c):
        m_copy(c).wait_recv()
        for i in range(SIDE):
            cols = pl.ds(i * PIECE, PIECE)
            ssum[c, i] = pse[c, k, :, cols] + mrecv[c, :, cols]
        for d in range(1, SIDE):
            l_copy(c, d).start()

    def stage7(c):
        for d in range(1, SIDE):
            l_copy(c, d).wait_recv()
        tot[c, 0] = (ssum[c, q] + lrecv[c, 0]) + (lrecv[c, 1] + lrecv[c, 2])
        for d in range(1, 8):
            b_copy(c, d).start()

    def stage8(c):
        for d in range(1, 8):
            b_copy(c, d).wait_recv()

        @pl.loop(0, 8)
        def _(d):
            src = (rep + 8 - d) % 8
            cols = pl.ds(pl.multiple_of((src % 2) * fh + c * WIDE + (src // 2) * PIECE, PIECE), PIECE)
            average = tot[c, d] / 8.0
            momentum_next = momentum_decay * par[4, :, cols] + average
            mn_ref[:, cols] = momentum_next
            gn_ref[:, cols] = par[3, :, cols] - outer_rate * (average + momentum_decay * momentum_next)

    stages = (stage0, stage1, stage2, stage3, stage4, stage5, stage6, stage7, stage8)

    @pl.loop(0, chunks + len(stages) - 1)
    def _(step):
        for lag, stage in enumerate(stages):
            c = step - lag

            @pl.when((c >= 0) & (c < chunks))
            def _():
                stage(c)

    @pl.loop(0, chunks)
    def _(c):
        for h in range(2):
            for p in range(2):
                for d in range(2):
                    for m in range(2):
                        xy_copy(c, h, p, d, m).wait_send()
        z_copy(c).wait_send()
        m_copy(c).wait_send()
        for d in range(1, SIDE):
            l_copy(c, d).wait_send()
        for d in range(1, 8):
            b_copy(c, d).wait_send()


def shards(
    tok_inputs, tok_grads, inner_params, adam_first, adam_second, global_params, outer_momentum
):
    ff = tok_grads.shape[-1]
    chunks = ff // 2 // WIDE
    out = jax.ShapeDtypeStruct((8, ff), jnp.float32)
    dma = pltpu.SemaphoreType.DMA
    vmem = pl.BlockSpec(memory_space=pltpu.VMEM)
    hbm = pl.BlockSpec(memory_space=pl.ANY)
    f32, b16 = jnp.float32, jnp.bfloat16
    first_moment, second_moment, global_next, momentum_next = pl.pallas_call(
        kernel,
        out_shape=(out,) * 4,
        in_specs=[vmem] + [hbm] * 6,
        out_specs=(vmem,) * 4,
        scratch_shapes=[
            pltpu.VMEM((2, 256, 256), b16),
            pltpu.VMEM((256, ff), b16),
            pltpu.VMEM((5, 8, ff), f32),
            pltpu.VMEM((SIDE, SIDE, 16, ff), f32),
            pltpu.VMEM((chunks, 2, 2, 3, SIDE, 16, HALF), b16),
            pltpu.VMEM((chunks, 2, 2, 3, SIDE, 16, HALF), b16),
            pltpu.VMEM((chunks, 2, 2, 3, 1, 16, HALF), b16),
            pltpu.VMEM((chunks, 2, 2, 3, 1, 16, HALF), b16),
            pltpu.VMEM((chunks, 16, WIDE), b16),
            pltpu.VMEM((chunks, 16, WIDE), b16),
            pltpu.VMEM((chunks, 2, 8, WIDE), f32),
            pltpu.VMEM((chunks, 8, WIDE), f32),
            pltpu.VMEM((chunks, SIDE, 8, PIECE), f32),
            pltpu.VMEM((chunks, SIDE - 1, 8, PIECE), f32),
            pltpu.VMEM((chunks, 8, 8, PIECE), f32),
            dma((chunks, 2)),
            dma((5,)),
            dma((chunks, 16)),
            dma((chunks, 16)),
            dma((chunks,)),
            dma((chunks,)),
            dma((chunks,)),
            dma((chunks,)),
            dma((chunks, SIDE - 1)),
            dma((chunks, SIDE - 1)),
            dma((chunks, 7)),
            dma((chunks, 7)),
        ],
        compiler_params=pltpu.CompilerParams(
            collective_id=0, has_side_effects=True, vmem_limit_bytes=60 * 2**20
        ),
        cost_estimate=pl.CostEstimate(
            flops=2 * 256 * 256 * ff, bytes_accessed=256 * ff * 2 + 9 * 8 * ff * 4, transcendentals=0
        ),
    )(
        tok_inputs[0], tok_grads[0], inner_params[0], adam_first[0], adam_second[0],
        global_params, outer_momentum,
    )
    return (first_moment[None], second_moment[None], global_next, momentum_next)


def solution(mesh):
    rows = P("fsdp", None)
    replicas = P("replica", "fsdp", None)
    return jax.shard_map(
        shards,
        mesh=mesh,
        in_specs=(replicas,) * 5 + (rows,) * 2,
        out_specs=(replicas, replicas, rows, rows),
        check_vma=False,
    )
```

```python
import functools
import jax
import jax.numpy as jnp
from jax import lax
from jax.experimental import pallas as pl
from jax.experimental.pallas import tpu as pltpu
from jax.sharding import PartitionSpec as P

beta_first = 0.9
beta_second = 0.95
inner_rate = 0.1
outer_rate = 0.7
momentum_decay = 0.9
epsilon = 1e-08
first_correction = 1.0 - 0.9**40
second_correction = 1.0 - 0.95**40

MESH = pl.DeviceIdType.MESH
SIDE = 4
WIDE = 1024
HALF = WIDE // 2
PIECE = WIDE // SIDE
POWER = 7
SCALES = (10, 8, 7)


def encode(value, stage):
    u = value * (2.0 ** SCALES[stage])
    u2 = u * u
    return (u2 * u2 * (u2 * u)).astype(jnp.bfloat16)


def decode_add(total, code, stage):
    y = code.astype(jnp.float32)
    size = jnp.exp2(jnp.log2(jnp.abs(y)) * (1.0 / POWER) - SCALES[stage])
    return jnp.where(y < 0, total - size, total + size)


def moments(first, second, gradient):
    first = beta_first * first + (1.0 - beta_first) * gradient
    second = beta_second * second + (1.0 - beta_second) * gradient * gradient
    return first, second


def sync_kernel(
    feat_ref, g_hbm, p_hbm, a1_hbm, a2_hbm, w_hbm,
    grad_ref, total_ref,
    feat_t, g_ref, par, part, s1a, s1b, r1a, r1b, s2a, s2b, r2a, r2b, sz, rz, pse, lrecv, tot,
    g_sem, par_sem, xy_send, xy_recv, z_send, z_recv, l_send, l_recv, b_send, b_recv,
):
    ff = g_ref.shape[1]
    fh = ff // 2
    chunks = fh // WIDE
    rep = lax.axis_index("replica")
    fs = lax.axis_index("fsdp")
    pos = (fs // 8, (fs // 2) % SIDE)
    zh = fs % 2
    zpeer = (rep, fs + 1 - 2 * zh)

    def ring(axis, step):
        y, x = pos
        if axis == 0:
            y = (y + step) % SIDE
        else:
            x = (x + step) % SIDE
        return (rep, y * 8 + x * 2 + zh)

    rings = [[ring(axis, step) for step in (1, SIDE - 1)] for axis in range(2)]
    near = [[(pos[axis] + step) % SIDE for step in range(SIDE)] for axis in range(2)]
    others = [(rep + d) % 8 for d in range(1, 8)]

    def start_col(c, h):
        return pl.multiple_of(h * fh + c * WIDE, WIDE)

    def g_copy(c, h):
        cols = pl.ds(start_col(c, h), WIDE)
        return pltpu.make_async_copy(g_hbm.at[:, cols], g_ref.at[:, cols], g_sem.at[c, h])

    par_copies = [
        pltpu.make_async_copy(src, par.at[i], par_sem.at[i])
        for i, src in enumerate((p_hbm, a1_hbm, a2_hbm, w_hbm))
    ]
    for h in range(2):
        g_copy(0, h).start()

    barrier = pltpu.get_barrier_semaphore()
    peers = rings[0] + rings[1] + [zpeer] + [(other, fs) for other in others]
    for peer in peers:
        pl.semaphore_signal(barrier, inc=1, device_id=peer, device_id_type=MESH)

    @pl.loop(1, chunks)
    def _(c):
        for h in range(2):
            g_copy(c, h).start()

    for copy in par_copies:
        copy.start()

    feat_t[0] = feat_ref[...].astype(jnp.float32).T.astype(jnp.bfloat16)
    for y in range(SIDE):
        for x in range(SIDE):
            feat_t[1, pl.ds((x * SIDE + y) * 16, 16), :] = feat_t[0, pl.ds((y * SIDE + x) * 16, 16), :]

    sends = ((s1a, s1b), (s2a, s2b))
    recvs = ((r1a, r1b), (r2a, r2b))

    def xy_start(c, p, m):
        for h in range(2):
            for d in range(2):
                pltpu.make_async_remote_copy(
                    src_ref=sends[p][m].at[c, h, d],
                    dst_ref=recvs[p][m].at[c, h, d],
                    send_sem=xy_send.at[2 * p + m],
                    recv_sem=xy_recv.at[c, 2 * p + m],
                    device_id=rings[(h + p) % 2][d],
                    device_id_type=MESH,
                ).start()

    def arrived(ref, sem):
        pltpu.make_async_copy(ref, ref, sem).wait()

    def z_copy(c):
        return pltpu.make_async_remote_copy(
            src_ref=sz.at[c], dst_ref=rz.at[c], send_sem=z_send.at[0], recv_sem=z_recv.at[c],
            device_id=zpeer, device_id_type=MESH,
        )

    def l_start(c):
        for i, other in enumerate(others):
            pltpu.make_async_remote_copy(
                src_ref=pse.at[c, other], dst_ref=lrecv.at[c, i],
                send_sem=l_send.at[0], recv_sem=l_recv.at[c],
                device_id=(other, fs), device_id_type=MESH,
            ).start()

    def b_start(c):
        for i, other in enumerate(others):
            pltpu.make_async_remote_copy(
                src_ref=tot.at[c, 0], dst_ref=tot.at[c, i + 1],
                send_sem=b_send.at[0], recv_sem=b_recv.at[c],
                device_id=(other, fs), device_id_type=MESH,
            ).start()

    def places(c, h, p):
        right = pl.ds(start_col(c, h), HALF)
        left = pl.ds(pl.multiple_of(start_col(c, h) + HALF, HALF), HALF)

        def at(dest, i, cols):
            return (dest, i, slice(None), cols) if p == 0 else (pos[h], dest, slice(None), cols)

        return near[(h + p) % 2], right, left, at

    def over_blocks(p, body):
        if p == 0:
            pl.loop(0, SIDE)(body)
        else:
            body(0)

    def first_sends(c, h, p):
        send = sends[p][0]
        j, right, left, at = places(c, h, p)

        def body(i):
            send[c, h, 0, 0, i] = encode(part[at(j[2], i, right)], p)
            send[c, h, 0, 1, i] = encode(part[at(j[1], i, left)], p)
            send[c, h, 1, 0, i] = encode(part[at(j[2], i, left)], p)
            send[c, h, 1, 1, i] = encode(part[at(j[3], i, right)], p)

        over_blocks(p, body)

    def second_sends(c, h, p):
        send, recv = sends[p][1], recvs[p][0]
        j, right, left, at = places(c, h, p)

        def body(i):
            send[c, h, 0, i] = encode(decode_add(part[at(j[1], i, right)], recv[c, h, 0, 0, i], p), p)
            send[c, h, 1, i] = encode(decode_add(part[at(j[3], i, left)], recv[c, h, 1, 0, i], p), p)

        over_blocks(p, body)

    def collect(c, h, p):
        near_recv, far_recv = recvs[p]
        j, right, left, at = places(c, h, p)

        def body(i):
            part[at(j[0], i, right)] = decode_add(
                decode_add(part[at(j[0], i, right)], far_recv[c, h, 0, i], p), near_recv[c, h, 1, 1, i], p
            )
            part[at(j[0], i, left)] = decode_add(
                decode_add(part[at(j[0], i, left)], near_recv[c, h, 0, 1, i], p), far_recv[c, h, 1, i], p
            )

        over_blocks(p, body)

    def multiply(c, h):
        g_copy(c, h).wait()

        @pl.loop(0, WIDE // 256)
        def _(t):
            cols = pl.ds(pl.multiple_of(start_col(c, h) + t * 256, 256), 256)
            part[:, :, :, cols] = jnp.dot(
                feat_t[h], g_ref[:, cols], preferred_element_type=jnp.float32
            ).reshape(SIDE, SIDE, 16, 256)

    def rows_of(h, whose, cols):
        return (pos[h], pos[1 - h], pl.ds(pl.multiple_of(whose * 8, 8), 8), cols)

    def stage0(c):
        for h in range(2):
            multiply(c, h)
            first_sends(c, h, 0)

        @pl.when(c == 0)
        def _():
            pl.semaphore_wait(barrier, len(peers))

        xy_start(c, 0, 0)

    def second_stage(c, p):
        arrived(recvs[p][0].at[c], xy_recv.at[c, 2 * p])
        for h in range(2):
            second_sends(c, h, p)
        xy_start(c, p, 1)

    def stage1(c):
        second_stage(c, 0)

    def stage2(c):
        arrived(r1b.at[c], xy_recv.at[c, 1])
        for h in range(2):
            collect(c, h, 0)
            first_sends(c, h, 1)
        xy_start(c, 1, 0)

    def stage3(c):
        second_stage(c, 1)

    def stage4(c):
        arrived(r2b.at[c], xy_recv.at[c, 3])
        for h in range(2):
            collect(c, h, 1)

        @pl.loop(0, WIDE // HALF)
        def _(t):
            both = [
                part[rows_of(h, 1 - zh, pl.ds(pl.multiple_of(start_col(c, h) + t * HALF, HALF), HALF))]
                for h in range(2)
            ]
            sz[c, :, pl.ds(pl.multiple_of(t * HALF, HALF), HALF)] = encode(jnp.concatenate(both, axis=0), 2)

        z_copy(c).start()

    def stage5(c):
        @pl.when(c == 0)
        def _():
            for copy in par_copies:
                copy.wait()

        z_copy(c).wait_recv()

        @pl.loop(0, SIDE)
        def _(t):
            sub = pl.ds(pl.multiple_of(t * PIECE, PIECE), PIECE)
            cols = [pl.ds(pl.multiple_of(start_col(c, h) + t * PIECE, PIECE), PIECE) for h in range(2)]
            both = jnp.concatenate([part[rows_of(h, zh, cols[h])] for h in range(2)], axis=0)
            both = decode_add(both, rz[c, :, sub], 2)
            for h in range(2):
                gradient = both[h * 8 : h * 8 + 8]
                grad_ref[:, cols[h]] = gradient
                first, second = moments(par[1, :, cols[h]], par[2, :, cols[h]], gradient)
                update = first / first_correction / (jnp.sqrt(second / second_correction) + epsilon)
                pse[c, 2 * t + h] = par[3, :, cols[h]] - (par[0, :, cols[h]] - inner_rate * update)

        l_start(c)

    def stage6(c):
        arrived(lrecv.at[c], l_recv.at[c])
        total = pse[c, rep]
        for i in range(7):
            total += lrecv[c, i]
        tot[c, 0] = total
        b_start(c)

    def stage7(c):
        arrived(tot.at[c, pl.ds(1, 7)], b_recv.at[c])

        @pl.loop(0, 8)
        def _(d):
            src = (rep + 8 - d) % 8
            cols = pl.ds(pl.multiple_of((src % 2) * fh + c * WIDE + (src // 2) * PIECE, PIECE), PIECE)
            total_ref[:, cols] = tot[c, d]

    stages = (stage0, stage1, stage2, stage3, stage4, stage5, stage6, stage7)

    @pl.loop(0, chunks + len(stages) - 1)
    def _(step):
        for lag, stage in enumerate(stages):
            c = step - lag

            @pl.when((c >= 0) & (c < chunks))
            def _():
                stage(c)

    for ref, sem in zip((s1a, s1b, s2a, s2b), range(4)):
        arrived(ref, xy_send.at[sem])
    arrived(sz, z_send.at[0])
    arrived(lrecv, l_send.at[0])
    arrived(lrecv, b_send.at[0])


def outer_kernel(grad_ref, total_ref, a1_ref, a2_ref, w_ref, m_ref, fm_ref, sm_ref, gn_ref, mn_ref):
    fm_ref[...], sm_ref[...] = moments(a1_ref[...], a2_ref[...], grad_ref[...])
    average = total_ref[...] / 8.0
    momentum_next = momentum_decay * m_ref[...] + average
    mn_ref[...] = momentum_next
    gn_ref[...] = w_ref[...] - outer_rate * (average + momentum_decay * momentum_next)


def shards(
    tok_inputs, tok_grads, inner_params, adam_first, adam_second, global_params, outer_momentum
):
    ff = tok_grads.shape[-1]
    chunks = ff // 2 // WIDE
    out = jax.ShapeDtypeStruct((8, ff), jnp.float32)
    dma = pltpu.SemaphoreType.DMA
    vmem = pl.BlockSpec(memory_space=pltpu.VMEM)
    hbm = pl.BlockSpec(memory_space=pl.ANY)
    f32, b16 = jnp.float32, jnp.bfloat16
    buffers = [
        pltpu.VMEM((chunks, 2, 2) + slots + (blocks, 16, HALF), b16)
        for blocks in (SIDE, 1)
        for _ in range(2)
        for slots in ((2,), ())
    ]
    gradient, total = pl.pallas_call(
        sync_kernel,
        out_shape=(out,) * 2,
        in_specs=[vmem] + [hbm] * 5,
        out_specs=(vmem,) * 2,
        scratch_shapes=[
            pltpu.VMEM((2, 256, 256), b16),
            pltpu.VMEM((256, ff), b16),
            pltpu.VMEM((4, 8, ff), f32),
            pltpu.VMEM((SIDE, SIDE, 16, ff), f32),
            *buffers,
            pltpu.VMEM((chunks, 16, WIDE), b16),
            pltpu.VMEM((chunks, 16, WIDE), b16),
            pltpu.VMEM((chunks, 8, 8, PIECE), f32),
            pltpu.VMEM((chunks, 7, 8, PIECE), f32),
            pltpu.VMEM((chunks, 8, 8, PIECE), f32),
            dma((chunks, 2)),
            dma((4,)),
            dma((4,)),
            dma((chunks, 4)),
            dma((1,)),
            dma((chunks,)),
            dma((1,)),
            dma((chunks,)),
            dma((1,)),
            dma((chunks,)),
        ],
        compiler_params=pltpu.CompilerParams(
            collective_id=0, has_side_effects=True, vmem_limit_bytes=56 * 2**20
        ),
        cost_estimate=pl.CostEstimate(
            flops=2 * 256 * 256 * ff, bytes_accessed=256 * ff * 2 + 6 * 8 * ff * 4, transcendentals=0
        ),
    )(tok_inputs[0], tok_grads[0], inner_params[0], adam_first[0], adam_second[0], global_params)
    first_moment, second_moment, global_next, momentum_next = pl.pallas_call(
        outer_kernel,
        out_shape=(out,) * 4,
        in_specs=[vmem] * 6,
        out_specs=(vmem,) * 4,
    )(gradient, total, adam_first[0], adam_second[0], global_params, outer_momentum)
    return (first_moment[None], second_moment[None], global_next, momentum_next)


def solution(mesh):
    rows = P("fsdp", None)
    replicas = P("replica", "fsdp", None)
    return jax.shard_map(
        shards,
        mesh=mesh,
        in_specs=(replicas,) * 5 + (rows,) * 2,
        out_specs=(replicas, replicas, rows, rows),
        check_vma=False,
    )
```

```python
import functools
import jax
import jax.numpy as jnp
from jax import lax
from jax.experimental import pallas as pl
from jax.experimental.pallas import tpu as pltpu
from jax.sharding import PartitionSpec as P

beta_first = 0.9
beta_second = 0.95
inner_rate = 0.1
outer_rate = 0.7
momentum_decay = 0.9
epsilon = 1e-08
first_correction = 1.0 - 0.9**40
second_correction = 1.0 - 0.95**40

MESH = pl.DeviceIdType.MESH
SIDE = 4
WIDE = 512
HALF = WIDE // 2
PIECE = WIDE // SIDE
POWER = 7
LAGS = (0, 2, 4, 6, 8, 11, 14)
SCALES = (10, 8, 7)


def encode(value, stage):
    u = value * (2.0 ** SCALES[stage])
    u2 = u * u
    return (u2 * u2 * (u2 * u)).astype(jnp.bfloat16)


def decode_add(total, code, stage):
    y = code.astype(jnp.float32)
    size = jnp.exp2(jnp.log2(jnp.abs(y)) * (1.0 / POWER) - SCALES[stage])
    return jnp.where(y < 0, total - size, total + size)


def moments(first, second, gradient):
    first = beta_first * first + (1.0 - beta_first) * gradient
    second = beta_second * second + (1.0 - beta_second) * gradient * gradient
    return first, second


def sync_kernel(
    feat_ref, g_hbm, p_hbm, a1_hbm, a2_hbm, w_hbm,
    grad_ref, tot,
    feat_t, g_ref, par, part, s1a, s1b, r1a, r1b, s2a, s2b, r2a, r2b, sz, rz, pse, lrecv,
    g_sem, par_sem, xy_send, xy_recv, z_send, z_recv, l_send, l_recv, b_send, b_recv,
):
    ff = g_ref.shape[1]
    fh = ff // 2
    chunks = fh // WIDE
    rep = lax.axis_index("replica")
    fs = lax.axis_index("fsdp")
    pos = (fs // 8, (fs // 2) % SIDE)
    zh = fs % 2
    zpeer = (rep, fs + 1 - 2 * zh)

    def ring(axis, step):
        y, x = pos
        if axis == 0:
            y = (y + step) % SIDE
        else:
            x = (x + step) % SIDE
        return (rep, y * 8 + x * 2 + zh)

    rings = [[ring(axis, step) for step in (1, SIDE - 1)] for axis in range(2)]
    near = [[(pos[axis] + step) % SIDE for step in range(SIDE)] for axis in range(2)]
    others = [(rep + d) % 8 for d in range(1, 8)]

    def start_col(c, h):
        return pl.multiple_of(h * fh + c * WIDE, WIDE)

    def g_copy(c, h):
        cols = pl.ds(start_col(c, h), WIDE)
        return pltpu.make_async_copy(g_hbm.at[:, cols], g_ref.at[:, cols], g_sem.at[c, h])

    par_copies = [
        pltpu.make_async_copy(src, par.at[i], par_sem.at[i])
        for i, src in enumerate((p_hbm, a1_hbm, a2_hbm, w_hbm))
    ]
    for h in range(2):
        g_copy(0, h).start()

    barrier = pltpu.get_barrier_semaphore()
    peers = rings[0] + rings[1] + [zpeer] + [(other, fs) for other in others]
    for peer in peers:
        pl.semaphore_signal(barrier, inc=1, device_id=peer, device_id_type=MESH)

    @pl.loop(1, chunks)
    def _(c):
        for h in range(2):
            g_copy(c, h).start()

    for copy in par_copies:
        copy.start()

    feat_t[0] = feat_ref[...].astype(jnp.float32).T.astype(jnp.bfloat16)
    for y in range(SIDE):
        for x in range(SIDE):
            feat_t[1, pl.ds((x * SIDE + y) * 16, 16), :] = feat_t[0, pl.ds((y * SIDE + x) * 16, 16), :]

    sends = ((s1a, s1b), (s2a, s2b))
    recvs = ((r1a, r1b), (r2a, r2b))

    def xy_start(c, p, m):
        for h in range(2):
            for d in range(2):
                pltpu.make_async_remote_copy(
                    src_ref=sends[p][m].at[c, h, d],
                    dst_ref=recvs[p][m].at[c, h, d],
                    send_sem=xy_send.at[2 * p + m],
                    recv_sem=xy_recv.at[c, 2 * p + m],
                    device_id=rings[(h + p) % 2][d],
                    device_id_type=MESH,
                ).start()

    def arrived(ref, sem):
        pltpu.make_async_copy(ref, ref, sem).wait()

    def z_copy(c):
        return pltpu.make_async_remote_copy(
            src_ref=sz.at[c], dst_ref=rz.at[c], send_sem=z_send.at[0], recv_sem=z_recv.at[c],
            device_id=zpeer, device_id_type=MESH,
        )

    def l_start(c):
        for i, other in enumerate(others):
            pltpu.make_async_remote_copy(
                src_ref=pse.at[c, other], dst_ref=lrecv.at[c, i],
                send_sem=l_send.at[0], recv_sem=l_recv.at[c],
                device_id=(other, fs), device_id_type=MESH,
            ).start()

    def b_start(c):
        for i, other in enumerate(others):
            pltpu.make_async_remote_copy(
                src_ref=tot.at[c, rep], dst_ref=tot.at[c, rep],
                send_sem=b_send.at[0], recv_sem=b_recv.at[0],
                device_id=(other, fs), device_id_type=MESH,
            ).start()

    def places(c, h, p):
        right = pl.ds(start_col(c, h), HALF)
        left = pl.ds(pl.multiple_of(start_col(c, h) + HALF, HALF), HALF)

        def at(dest, i, cols):
            return (dest, i, slice(None), cols) if p == 0 else (pos[h], dest, slice(None), cols)

        return near[(h + p) % 2], right, left, at

    def over_blocks(p, body):
        if p == 0:
            pl.loop(0, SIDE)(body)
        else:
            body(0)

    def first_sends(c, h, p):
        send = sends[p][0]
        j, right, left, at = places(c, h, p)

        def body(i):
            send[c, h, 0, 0, i] = encode(part[at(j[2], i, right)], p)
            send[c, h, 0, 1, i] = encode(part[at(j[1], i, left)], p)
            send[c, h, 1, 0, i] = encode(part[at(j[2], i, left)], p)
            send[c, h, 1, 1, i] = encode(part[at(j[3], i, right)], p)

        over_blocks(p, body)

    def second_sends(c, h, p):
        send, recv = sends[p][1], recvs[p][0]
        j, right, left, at = places(c, h, p)

        def body(i):
            send[c, h, 0, i] = encode(decode_add(part[at(j[1], i, right)], recv[c, h, 0, 0, i], p), p)
            send[c, h, 1, i] = encode(decode_add(part[at(j[3], i, left)], recv[c, h, 1, 0, i], p), p)

        over_blocks(p, body)

    def collect(c, h, p):
        near_recv, far_recv = recvs[p]
        j, right, left, at = places(c, h, p)

        def body(i):
            part[at(j[0], i, right)] = decode_add(
                decode_add(part[at(j[0], i, right)], far_recv[c, h, 0, i], p), near_recv[c, h, 1, 1, i], p
            )
            part[at(j[0], i, left)] = decode_add(
                decode_add(part[at(j[0], i, left)], near_recv[c, h, 0, 1, i], p), far_recv[c, h, 1, i], p
            )

        over_blocks(p, body)

    def multiply(c, h):
        g_copy(c, h).wait()

        @pl.loop(0, WIDE // 256)
        def _(t):
            cols = pl.ds(pl.multiple_of(start_col(c, h) + t * 256, 256), 256)
            part[:, :, :, cols] = jnp.dot(
                feat_t[h], g_ref[:, cols], preferred_element_type=jnp.float32
            ).reshape(SIDE, SIDE, 16, 256)

    def rows_of(h, whose, cols):
        return (pos[h], pos[1 - h], pl.ds(pl.multiple_of(whose * 8, 8), 8), cols)

    def stage0(c):
        for h in range(2):
            multiply(c, h)
            first_sends(c, h, 0)

        @pl.when(c == 0)
        def _():
            pl.semaphore_wait(barrier, len(peers))

        xy_start(c, 0, 0)

    def second_stage(c, p):
        arrived(recvs[p][0].at[c], xy_recv.at[c, 2 * p])
        for h in range(2):
            second_sends(c, h, p)
        xy_start(c, p, 1)

    def stage1(c):
        second_stage(c, 0)

    def stage2(c):
        arrived(r1b.at[c], xy_recv.at[c, 1])
        for h in range(2):
            collect(c, h, 0)
            first_sends(c, h, 1)
        xy_start(c, 1, 0)

    def stage3(c):
        second_stage(c, 1)

    def stage4(c):
        arrived(r2b.at[c], xy_recv.at[c, 3])
        for h in range(2):
            collect(c, h, 1)

        @pl.loop(0, WIDE // HALF)
        def _(t):
            both = [
                part[rows_of(h, 1 - zh, pl.ds(pl.multiple_of(start_col(c, h) + t * HALF, HALF), HALF))]
                for h in range(2)
            ]
            sz[c, :, pl.ds(pl.multiple_of(t * HALF, HALF), HALF)] = encode(jnp.concatenate(both, axis=0), 2)

        z_copy(c).start()

    def stage5(c):
        @pl.when(c == 0)
        def _():
            for copy in par_copies:
                copy.wait()

        z_copy(c).wait_recv()

        @pl.loop(0, SIDE)
        def _(t):
            sub = pl.ds(pl.multiple_of(t * PIECE, PIECE), PIECE)
            cols = [pl.ds(pl.multiple_of(start_col(c, h) + t * PIECE, PIECE), PIECE) for h in range(2)]
            both = jnp.concatenate([part[rows_of(h, zh, cols[h])] for h in range(2)], axis=0)
            both = decode_add(both, rz[c, :, sub], 2)
            for h in range(2):
                gradient = both[h * 8 : h * 8 + 8]
                grad_ref[:, cols[h]] = gradient
                first, second = moments(par[1, :, cols[h]], par[2, :, cols[h]], gradient)
                update = first / first_correction / (jnp.sqrt(second / second_correction) + epsilon)
                pse[c, 2 * t + h] = par[3, :, cols[h]] - (par[0, :, cols[h]] - inner_rate * update)

        l_start(c)

    def stage6(c):
        arrived(lrecv.at[c], l_recv.at[c])
        total = pse[c, rep]
        for i in range(7):
            total += lrecv[c, i]
        tot[c, rep] = total
        b_start(c)

    stages = (stage0, stage1, stage2, stage3, stage4, stage5, stage6)

    @pl.loop(0, chunks + LAGS[-1])
    def _(step):
        for lag, stage in zip(LAGS, stages):
            c = step - lag

            @pl.when((c >= 0) & (c < chunks))
            def _():
                stage(c)

    for ref, sem in zip((s1a, s1b, s2a, s2b), range(4)):
        arrived(ref, xy_send.at[sem])
    arrived(sz, z_send.at[0])
    arrived(lrecv, l_send.at[0])
    arrived(lrecv, b_send.at[0])
    arrived(lrecv, b_recv.at[0])


def outer_kernel(grad_ref, tot_ref, a1_ref, a2_ref, w_ref, m_ref, fm_ref, sm_ref, gn_ref, mn_ref):
    fm_ref[...], sm_ref[...] = moments(a1_ref[...], a2_ref[...], grad_ref[...])
    chunks, owners, _, piece = tot_ref.shape
    for c in range(chunks):
        for owner in range(owners):
            start = (owner % 2) * chunks * WIDE + c * WIDE + (owner // 2) * piece
            cols = pl.ds(start, piece)
            average = tot_ref[c, owner] / 8.0
            momentum_next = momentum_decay * m_ref[:, cols] + average
            mn_ref[:, cols] = momentum_next
            gn_ref[:, cols] = w_ref[:, cols] - outer_rate * (average + momentum_decay * momentum_next)


def shards(
    tok_inputs, tok_grads, inner_params, adam_first, adam_second, global_params, outer_momentum
):
    ff = tok_grads.shape[-1]
    chunks = ff // 2 // WIDE
    out = jax.ShapeDtypeStruct((8, ff), jnp.float32)
    dma = pltpu.SemaphoreType.DMA
    vmem = pl.BlockSpec(memory_space=pltpu.VMEM)
    hbm = pl.BlockSpec(memory_space=pl.ANY)
    f32, b16 = jnp.float32, jnp.bfloat16
    buffers = [
        pltpu.VMEM((chunks, 2, 2) + slots + (blocks, 16, HALF), b16)
        for blocks in (SIDE, 1)
        for _ in range(2)
        for slots in ((2,), ())
    ]
    gradient, total = pl.pallas_call(
        sync_kernel,
        out_shape=(out, jax.ShapeDtypeStruct((chunks, 8, 8, PIECE), f32)),
        in_specs=[vmem] + [hbm] * 5,
        out_specs=(vmem,) * 2,
        scratch_shapes=[
            pltpu.VMEM((2, 256, 256), b16),
            pltpu.VMEM((256, ff), b16),
            pltpu.VMEM((4, 8, ff), f32),
            pltpu.VMEM((SIDE, SIDE, 16, ff), f32),
            *buffers,
            pltpu.VMEM((chunks, 16, WIDE), b16),
            pltpu.VMEM((chunks, 16, WIDE), b16),
            pltpu.VMEM((chunks, 8, 8, PIECE), f32),
            pltpu.VMEM((chunks, 7, 8, PIECE), f32),
            dma((chunks, 2)),
            dma((4,)),
            dma((4,)),
            dma((chunks, 4)),
            dma((1,)),
            dma((chunks,)),
            dma((1,)),
            dma((chunks,)),
            dma((1,)),
            dma((1,)),
        ],
        compiler_params=pltpu.CompilerParams(
            collective_id=0, has_side_effects=True, vmem_limit_bytes=56 * 2**20
        ),
        cost_estimate=pl.CostEstimate(
            flops=2 * 256 * 256 * ff, bytes_accessed=256 * ff * 2 + 6 * 8 * ff * 4, transcendentals=0
        ),
    )(tok_inputs[0], tok_grads[0], inner_params[0], adam_first[0], adam_second[0], global_params)
    first_moment, second_moment, global_next, momentum_next = pl.pallas_call(
        outer_kernel,
        out_shape=(out,) * 4,
        in_specs=[vmem] * 6,
        out_specs=(vmem,) * 4,
    )(gradient, total, adam_first[0], adam_second[0], global_params, outer_momentum)
    return (first_moment[None], second_moment[None], global_next, momentum_next)


def solution(mesh):
    rows = P("fsdp", None)
    replicas = P("replica", "fsdp", None)
    return jax.shard_map(
        shards,
        mesh=mesh,
        in_specs=(replicas,) * 5 + (rows,) * 2,
        out_specs=(replicas, replicas, rows, rows),
        check_vma=False,
    )
```

```python
import functools
import jax
import jax.numpy as jnp
from jax import lax
from jax.experimental import pallas as pl
from jax.experimental.pallas import tpu as pltpu
from jax.sharding import PartitionSpec as P

beta_first = 0.9
beta_second = 0.95
inner_rate = 0.1
outer_rate = 0.7
momentum_decay = 0.9
epsilon = 1e-08
first_correction = 1.0 - 0.9**40
second_correction = 1.0 - 0.95**40

MESH = pl.DeviceIdType.MESH
SIDE = 4
WIDE = 512
HALF = WIDE // 2
PIECE = WIDE // SIDE
POWER = 7
LAGS = (0, 2, 4, 6, 8, 11, 14)
SCALES = (10, 8, 7)


def encode(value, stage):
    u = value * (2.0 ** SCALES[stage])
    u2 = u * u
    return (u2 * u2 * (u2 * u)).astype(jnp.bfloat16)


def decode_add(total, code, stage):
    y = code.astype(jnp.float32)
    size = jnp.exp2(jnp.log2(jnp.abs(y)) * (1.0 / POWER) - SCALES[stage])
    return jnp.where(y < 0, total - size, total + size)


def moments(first, second, gradient):
    first = beta_first * first + (1.0 - beta_first) * gradient
    second = beta_second * second + (1.0 - beta_second) * gradient * gradient
    return first, second


def sync_kernel(
    feat_ref, g_hbm, p_hbm, a1_hbm, a2_hbm, w_hbm,
    grad_ref, tot,
    feat_t, g_ref, par, part, s1a, s1b, r1a, r1b, s2a, s2b, r2a, r2b, sz, rz, pse, lrecv,
    g_sem, par_sem, xy_send, xy_recv, z_send, z_recv, l_send, l_recv, b_send, b_recv,
):
    ff = g_ref.shape[1]
    fh = ff // 2
    chunks = fh // WIDE
    rep = lax.axis_index("replica")
    fs = lax.axis_index("fsdp")
    pos = (fs // 8, (fs // 2) % SIDE)
    zh = fs % 2
    zpeer = (rep, fs + 1 - 2 * zh)

    def ring(axis, step):
        y, x = pos
        if axis == 0:
            y = (y + step) % SIDE
        else:
            x = (x + step) % SIDE
        return (rep, y * 8 + x * 2 + zh)

    rings = [[ring(axis, step) for step in (1, SIDE - 1)] for axis in range(2)]
    near = [[(pos[axis] + step) % SIDE for step in range(SIDE)] for axis in range(2)]
    others = [(rep + d) % 8 for d in range(1, 8)]

    def start_col(c, h):
        return pl.multiple_of(h * fh + c * WIDE, WIDE)

    def g_copy(c, h):
        cols = pl.ds(start_col(c, h), WIDE)
        return pltpu.make_async_copy(g_hbm.at[:, cols], g_ref.at[:, cols], g_sem.at[c, h])

    par_copies = [
        pltpu.make_async_copy(src, par.at[i], par_sem.at[i])
        for i, src in enumerate((p_hbm, a1_hbm, a2_hbm, w_hbm))
    ]
    for h in range(2):
        g_copy(0, h).start()

    barrier = pltpu.get_barrier_semaphore()
    peers = rings[0] + rings[1] + [zpeer] + [(other, fs) for other in others]
    for peer in peers:
        pl.semaphore_signal(barrier, inc=1, device_id=peer, device_id_type=MESH)

    @pl.loop(1, chunks)
    def _(c):
        for h in range(2):
            g_copy(c, h).start()

    for copy in par_copies:
        copy.start()

    feat_t[0] = feat_ref[...].astype(jnp.float32).T.astype(jnp.bfloat16)
    for y in range(SIDE):
        for x in range(SIDE):
            feat_t[1, pl.ds((x * SIDE + y) * 16, 16), :] = feat_t[0, pl.ds((y * SIDE + x) * 16, 16), :]

    sends = ((s1a, s1b), (s2a, s2b))
    recvs = ((r1a, r1b), (r2a, r2b))

    def xy_start(c, p, m):
        for h in range(2):
            for d in range(2):
                pltpu.make_async_remote_copy(
                    src_ref=sends[p][m].at[c, h, d],
                    dst_ref=recvs[p][m].at[c, h, d],
                    send_sem=xy_send.at[2 * p + m],
                    recv_sem=xy_recv.at[c, 2 * p + m],
                    device_id=rings[(h + p) % 2][d],
                    device_id_type=MESH,
                ).start()

    def arrived(ref, sem):
        pltpu.make_async_copy(ref, ref, sem).wait()

    def z_copy(c):
        return pltpu.make_async_remote_copy(
            src_ref=sz.at[c], dst_ref=rz.at[c], send_sem=z_send.at[0], recv_sem=z_recv.at[c],
            device_id=zpeer, device_id_type=MESH,
        )

    def l_start(c):
        for i, other in enumerate(others):
            pltpu.make_async_remote_copy(
                src_ref=pse.at[c, other], dst_ref=lrecv.at[c, i],
                send_sem=l_send.at[0], recv_sem=l_recv.at[c],
                device_id=(other, fs), device_id_type=MESH,
            ).start()

    def b_start(c):
        for i, other in enumerate(others):
            pltpu.make_async_remote_copy(
                src_ref=tot.at[c, rep], dst_ref=tot.at[c, rep],
                send_sem=b_send.at[0], recv_sem=b_recv.at[0],
                device_id=(other, fs), device_id_type=MESH,
            ).start()

    def places(c, h, p):
        right = pl.ds(start_col(c, h), HALF)
        left = pl.ds(pl.multiple_of(start_col(c, h) + HALF, HALF), HALF)

        def at(dest, i, cols):
            return (dest, i, slice(None), cols) if p == 0 else (pos[h], dest, slice(None), cols)

        return near[(h + p) % 2], right, left, at

    def over_blocks(p, body):
        if p == 0:
            pl.loop(0, SIDE)(body)
        else:
            body(0)

    def first_sends(c, h, p):
        send = sends[p][0]
        j, right, left, at = places(c, h, p)

        def body(i):
            send[c, h, 0, 0, i] = encode(part[at(j[2], i, right)], p)
            send[c, h, 0, 1, i] = encode(part[at(j[1], i, left)], p)
            send[c, h, 1, 0, i] = encode(part[at(j[2], i, left)], p)
            send[c, h, 1, 1, i] = encode(part[at(j[3], i, right)], p)

        over_blocks(p, body)

    def second_sends(c, h, p):
        send, recv = sends[p][1], recvs[p][0]
        j, right, left, at = places(c, h, p)

        def body(i):
            send[c, h, 0, i] = encode(decode_add(part[at(j[1], i, right)], recv[c, h, 0, 0, i], p), p)
            send[c, h, 1, i] = encode(decode_add(part[at(j[3], i, left)], recv[c, h, 1, 0, i], p), p)

        over_blocks(p, body)

    def collect(c, h, p):
        near_recv, far_recv = recvs[p]
        j, right, left, at = places(c, h, p)

        def body(i):
            part[at(j[0], i, right)] = decode_add(
                decode_add(part[at(j[0], i, right)], far_recv[c, h, 0, i], p), near_recv[c, h, 1, 1, i], p
            )
            part[at(j[0], i, left)] = decode_add(
                decode_add(part[at(j[0], i, left)], near_recv[c, h, 0, 1, i], p), far_recv[c, h, 1, i], p
            )

        over_blocks(p, body)

    def multiply(c, h):
        g_copy(c, h).wait()

        @pl.loop(0, WIDE // 256)
        def _(t):
            cols = pl.ds(pl.multiple_of(start_col(c, h) + t * 256, 256), 256)
            part[:, :, :, cols] = jnp.dot(
                feat_t[h], g_ref[:, cols], preferred_element_type=jnp.float32
            ).reshape(SIDE, SIDE, 16, 256)

    def rows_of(h, whose, cols):
        return (pos[h], pos[1 - h], pl.ds(pl.multiple_of(whose * 8, 8), 8), cols)

    def stage0(c):
        for h in range(2):
            multiply(c, h)
            first_sends(c, h, 0)

        @pl.when(c == 0)
        def _():
            pl.semaphore_wait(barrier, len(peers))

        xy_start(c, 0, 0)

    def second_stage(c, p):
        arrived(recvs[p][0].at[c], xy_recv.at[c, 2 * p])
        for h in range(2):
            second_sends(c, h, p)
        xy_start(c, p, 1)

    def stage1(c):
        second_stage(c, 0)

    def stage2(c):
        arrived(r1b.at[c], xy_recv.at[c, 1])
        for h in range(2):
            collect(c, h, 0)
            first_sends(c, h, 1)
        xy_start(c, 1, 0)

    def stage3(c):
        second_stage(c, 1)

    def stage4(c):
        arrived(r2b.at[c], xy_recv.at[c, 3])
        for h in range(2):
            collect(c, h, 1)

        @pl.loop(0, WIDE // HALF)
        def _(t):
            both = [
                part[rows_of(h, 1 - zh, pl.ds(pl.multiple_of(start_col(c, h) + t * HALF, HALF), HALF))]
                for h in range(2)
            ]
            sz[c, :, pl.ds(pl.multiple_of(t * HALF, HALF), HALF)] = encode(jnp.concatenate(both, axis=0), 2)

        z_copy(c).start()

    def stage5(c):
        @pl.when(c == 0)
        def _():
            for copy in par_copies:
                copy.wait()

        z_copy(c).wait_recv()

        @pl.loop(0, SIDE)
        def _(t):
            sub = pl.ds(pl.multiple_of(t * PIECE, PIECE), PIECE)
            cols = [pl.ds(pl.multiple_of(start_col(c, h) + t * PIECE, PIECE), PIECE) for h in range(2)]
            both = jnp.concatenate([part[rows_of(h, zh, cols[h])] for h in range(2)], axis=0)
            both = decode_add(both, rz[c, :, sub], 2)
            for h in range(2):
                gradient = both[h * 8 : h * 8 + 8]
                grad_ref[:, cols[h]] = gradient
                first, second = moments(par[1, :, cols[h]], par[2, :, cols[h]], gradient)
                update = first / first_correction / (jnp.sqrt(second / second_correction) + epsilon)
                pse[c, 2 * t + h] = par[3, :, cols[h]] - (par[0, :, cols[h]] - inner_rate * update)

        l_start(c)

    def stage6(c):
        arrived(lrecv.at[c], l_recv.at[c])
        total = pse[c, rep]
        for i in range(7):
            total += lrecv[c, i]
        tot[c, rep] = total
        b_start(c)

    stages = (stage0, stage1, stage2, stage3, stage4, stage5, stage6)

    @pl.loop(0, chunks + LAGS[-1])
    def _(step):
        for n in (0, 6, 5, 1, 2, 3, 4):
            lag, stage = LAGS[n], stages[n]
            c = step - lag

            @pl.when((c >= 0) & (c < chunks))
            def _():
                stage(c)

    for ref, sem in zip((s1a, s1b, s2a, s2b), range(4)):
        arrived(ref, xy_send.at[sem])
    arrived(sz, z_send.at[0])
    arrived(lrecv, l_send.at[0])
    arrived(lrecv, b_send.at[0])
    arrived(lrecv, b_recv.at[0])


def outer_kernel(grad_ref, tot_ref, a1_ref, a2_ref, w_ref, m_ref, fm_ref, sm_ref, gn_ref, mn_ref):
    fm_ref[...], sm_ref[...] = moments(a1_ref[...], a2_ref[...], grad_ref[...])
    chunks, quarters, _, _, piece = tot_ref.shape
    for c in range(chunks):
        for quarter in range(quarters):
            cols = pl.ds(c * WIDE + quarter * piece, piece)
            average = tot_ref[c, quarter, 0] / 8.0
            momentum_next = momentum_decay * m_ref[:, cols] + average
            mn_ref[:, cols] = momentum_next
            gn_ref[:, cols] = w_ref[:, cols] - outer_rate * (average + momentum_decay * momentum_next)


def shards(
    tok_inputs, tok_grads, inner_params, adam_first, adam_second, global_params, outer_momentum
):
    ff = tok_grads.shape[-1]
    chunks = ff // 2 // WIDE
    out = jax.ShapeDtypeStruct((8, ff), jnp.float32)
    dma = pltpu.SemaphoreType.DMA
    vmem = pl.BlockSpec(memory_space=pltpu.VMEM)
    hbm = pl.BlockSpec(memory_space=pl.ANY)
    half = pl.BlockSpec((8, ff // 2), lambda h: (0, h))
    f32, b16 = jnp.float32, jnp.bfloat16
    buffers = [
        pltpu.VMEM((chunks, 2, 2) + slots + (blocks, 16, HALF), b16)
        for blocks in (SIDE, 1)
        for _ in range(2)
        for slots in ((2,), ())
    ]
    gradient, total = pl.pallas_call(
        sync_kernel,
        out_shape=(out, jax.ShapeDtypeStruct((chunks, 8, 8, PIECE), f32)),
        in_specs=[vmem] + [hbm] * 5,
        out_specs=(vmem,) * 2,
        scratch_shapes=[
            pltpu.VMEM((2, 256, 256), b16),
            pltpu.VMEM((256, ff), b16),
            pltpu.VMEM((4, 8, ff), f32),
            pltpu.VMEM((SIDE, SIDE, 16, ff), f32),
            *buffers,
            pltpu.VMEM((chunks, 16, WIDE), b16),
            pltpu.VMEM((chunks, 16, WIDE), b16),
            pltpu.VMEM((chunks, 8, 8, PIECE), f32),
            pltpu.VMEM((chunks, 7, 8, PIECE), f32),
            dma((chunks, 2)),
            dma((4,)),
            dma((4,)),
            dma((chunks, 4)),
            dma((1,)),
            dma((chunks,)),
            dma((1,)),
            dma((chunks,)),
            dma((1,)),
            dma((1,)),
        ],
        compiler_params=pltpu.CompilerParams(
            collective_id=0, has_side_effects=True, vmem_limit_bytes=56 * 2**20
        ),
        cost_estimate=pl.CostEstimate(
            flops=2 * 256 * 256 * ff, bytes_accessed=256 * ff * 2 + 6 * 8 * ff * 4, transcendentals=0
        ),
    )(tok_inputs[0], tok_grads[0], inner_params[0], adam_first[0], adam_second[0], global_params)
    first_moment, second_moment, global_next, momentum_next = pl.pallas_call(
        outer_kernel,
        out_shape=(out,) * 4,
        grid=(2,),
        in_specs=[half, pl.BlockSpec((chunks, SIDE, 1, 8, PIECE), lambda h: (0, 0, h, 0, 0))] + [half] * 4,
        out_specs=(half,) * 4,
    )(gradient, total.reshape(chunks, SIDE, 2, 8, PIECE), adam_first[0], adam_second[0], global_params, outer_momentum)
    return (first_moment[None], second_moment[None], global_next, momentum_next)


def solution(mesh):
    rows = P("fsdp", None)
    replicas = P("replica", "fsdp", None)
    return jax.shard_map(
        shards,
        mesh=mesh,
        in_specs=(replicas,) * 5 + (rows,) * 2,
        out_specs=(replicas, replicas, rows, rows),
        check_vma=False,
    )
```
